32 devices in a mesh: req: 4 (over y, x), seq: 8 (over z, core).
Axes of the slice: x: 2, y: 2, z: 4, core: 2. Of those that a mesh axis runs over, the one named last changes fastest.
Arguments:
- sequence_sizes: int32 [4], P('req'), may hold values from 128 to 2048, as said below
- acceptor: bfloat16 [4, 2048, 2048], P('req', 'seq'), may hold values from -6 to 6
- fading_scores: bfloat16 [4, 2048, 2048], P('req', 'seq'), may hold values from -20 to 6
- address_source: bfloat16 [4, 2048, 2048], P('req', 'seq'), may hold values from -6 to 6
- payload_source: bfloat16 [4, 2048, 2048], P('req', 'seq'), may hold values from -40 to 40
- learning_speed_scores: bfloat16 [4, 2048, 2048], P('req', 'seq'), may hold values from -20 to 6
- exit_switch: bfloat16 [4, 2048, 2048], P('req', 'seq'), may hold values from -6 to 6
- address_removal_factor: float32 [2048], replicated, may hold values from 0.4 to 1.6
- address_learning_factor: float32 [2048], replicated, may hold values from 0.3 to 1.5
- present_extra_factor: float32 [2048], replicated, may hold values from -0.9 to 0.9
- cluster_scale_term: float32 [2048], replicated, may hold values from 0.1 to 1.9
- cluster_shift_term: float32 [2048], replicated, may hold values from -1.8 to 1.8
- final_projection: bfloat16 [2048, 4096], P(('req', 'seq')), may hold values from -0.125 to 0.125
Outputs:
- mixed_out: bfloat16 [4, 2048, 4096], P('req', 'seq')
The draws below stay inside these ranges and needn't reach their ends.
Inputs may be any that keep to these rules, and one draw needn't show every extreme that they name: `sequence_sizes`: each length is a multiple of 128, and in every draw some request has all 2048 tokens.
All inputs are finite; a program needn't handle non-finite values.
Results may differ from the reference program's by a relative error of at most 0.0049.
Values may be sent and summed in bfloat16 or wider, within the bound.
A program may use at most 256 MiB of HBM per device.

```python
import math
import jax
import jax.numpy as jnp
from jax import lax

MODEL_WIDTH = 4096
PER_UNIT_WIDTH = 64
LOCAL_UNITS = 32
TOK_DEV = 256
LENGTH_STEP = 128
ALL_UNITS_WIDTH = 2048
REQUEST_COUNT = 4
TOKEN_SLOTS = 2048


DECAY_SCALE = 0.606531


def slow_heads(key, slow_share):
    return jax.random.bernoulli(key, slow_share, (REQUEST_COUNT, 1, LOCAL_UNITS, 1))


def draw_fading_scores(key, part):
    slow_share = 0.5
    slow_head_mask = slow_heads(key, slow_share)
    key = jax.random.fold_in(key, 3)
    random_subkeys = jax.random.split(key, 5)
    scale_u = jnp.exp(jax.random.uniform(random_subkeys[0], (REQUEST_COUNT, 1, LOCAL_UNITS, PER_UNIT_WIDTH), jnp.float32, jnp.log(0.2), jnp.log(1.0)))
    slow_logit = jnp.log(scale_u / (DECAY_SCALE * TOKEN_SLOTS))
    fast_logit = jax.random.uniform(random_subkeys[1], (REQUEST_COUNT, 1, LOCAL_UNITS, PER_UNIT_WIDTH), jnp.float32, -3.4, 3.0)
    base_logit = jnp.where(slow_head_mask, slow_logit, fast_logit)
    device_shift = jax.random.uniform(random_subkeys[2], (REQUEST_COUNT, TOKEN_SLOTS // TOK_DEV, LOCAL_UNITS, 1), jnp.float32, -0.7, 0.7)
    device_shift = jnp.repeat(device_shift, TOK_DEV, axis=1)
    noise_term = 0.5 * jax.random.normal(random_subkeys[3], (REQUEST_COUNT, TOKEN_SLOTS, LOCAL_UNITS, PER_UNIT_WIDTH), jnp.float32)
    logit_values = base_logit + device_shift + noise_term
    spike_position = jax.random.randint(random_subkeys[4], (REQUEST_COUNT, 2), 0, TOKEN_SLOTS)
    spike_flag = jnp.any(jnp.arange(TOKEN_SLOTS)[None, :, None] == spike_position[:, None, :], -1)
    logit_values = jnp.where(spike_flag[:, :, None, None] & slow_head_mask, 1.0, logit_values)
    logit_values = jnp.clip(logit_values, -20.0, 6.0)
    return logit_values.reshape(REQUEST_COUNT, TOKEN_SLOTS, LOCAL_UNITS * PER_UNIT_WIDTH).astype(jnp.bfloat16)


def draw_learning_speed_scores(key, part):
    slow_share = 0.5
    slow_head_mask = slow_heads(key, slow_share)
    key = jax.random.fold_in(key, 5)
    random_subkeys = jax.random.split(key, 3)
    scale_c = jnp.exp(jax.random.uniform(random_subkeys[0], (REQUEST_COUNT, 1, LOCAL_UNITS, PER_UNIT_WIDTH), jnp.float32, 0.0, jnp.log(8.0)))
    slow_logit = jnp.log(scale_c / TOKEN_SLOTS)
    fast_logit = jax.random.uniform(random_subkeys[1], (REQUEST_COUNT, 1, LOCAL_UNITS, PER_UNIT_WIDTH), jnp.float32, -2.0, 3.0)
    noise_term = 0.5 * jax.random.normal(random_subkeys[2], (REQUEST_COUNT, TOKEN_SLOTS, LOCAL_UNITS, PER_UNIT_WIDTH), jnp.float32)
    logit_values = jnp.clip(jnp.where(slow_head_mask, slow_logit, fast_logit) + noise_term, -20.0, 6.0)
    return logit_values.reshape(REQUEST_COUNT, TOKEN_SLOTS, LOCAL_UNITS * PER_UNIT_WIDTH).astype(jnp.bfloat16)


def draw_payload_source(key, part):
    key = jax.random.fold_in(key, 7)
    random_subkeys = jax.random.split(key, 3)
    channel_scale = jnp.exp(jax.random.uniform(random_subkeys[0], (1, 1, LOCAL_UNITS * PER_UNIT_WIDTH), jnp.float32, jnp.log(0.3), jnp.log(3.0)))
    row_scale = jnp.exp(jax.random.uniform(random_subkeys[1], (REQUEST_COUNT, TOKEN_SLOTS, 1), jnp.float32, jnp.log(0.3), jnp.log(3.0)))
    base_vals = jax.random.normal(random_subkeys[2], (REQUEST_COUNT, TOKEN_SLOTS, LOCAL_UNITS * PER_UNIT_WIDTH), jnp.float32)
    return jnp.clip(base_vals * channel_scale * row_scale, -40.0, 40.0).astype(jnp.bfloat16)


def draw_sequence_sizes(key, part):
    key = jax.random.fold_in(key, 9)
    random_subkeys = jax.random.split(key, 2)
    steps_all = TOKEN_SLOTS // LENGTH_STEP
    counts_drawn = jax.random.randint(random_subkeys[0], (REQUEST_COUNT,), 1, steps_all + 1)
    longest = jax.random.randint(random_subkeys[1], (), 0, REQUEST_COUNT)
    counts_drawn = jnp.where(jnp.arange(REQUEST_COUNT) == longest, steps_all, counts_drawn)
    return (counts_drawn * LENGTH_STEP).astype(jnp.int32)


def steps_of(stream_key, shape, cuts, least, top_value):
    loudness, own = 1.0, jax.random.fold_in(stream_key, 6)
    for dim, blocks in cuts:
        steps = jnp.exp(jax.random.uniform(jax.random.fold_in(own, dim), (blocks,), jnp.float32, least / len(cuts), top_value / len(cuts)))
        loudness = loudness * jnp.repeat(steps, shape[dim] // blocks).reshape([-1 if axis == dim else 1 for axis in range(len(shape))])
    return loudness


def normal_values(own_key, dims, deviation, reach, cuts=(), kind=jnp.bfloat16):
    level = steps_of(own_key, dims, cuts, -0.22, 0.18) if cuts else 1.0
    values = jax.random.normal(own_key, dims, jnp.float32) * deviation * level
    return jnp.minimum(jnp.maximum(values, -reach), reach).astype(kind)


def setup_inputs(seed: int = 0) -> dict:
    streams_of = jax.random.split(jax.random.key(seed), 14)
    return {
        "sequence_sizes": draw_sequence_sizes(jax.random.fold_in(streams_of[13], 71), 0),
        "acceptor": normal_values(streams_of[1], (REQUEST_COUNT, TOKEN_SLOTS, ALL_UNITS_WIDTH), 1.0, 6.0, ((0, 4), (1, 8))),
        "fading_scores": draw_fading_scores(jax.random.fold_in(streams_of[13], 71), 0),
        "address_source": normal_values(streams_of[3], (REQUEST_COUNT, TOKEN_SLOTS, ALL_UNITS_WIDTH), 1.0, 6.0, ((0, 4), (1, 8))),
        "payload_source": draw_payload_source(jax.random.fold_in(streams_of[13], 71), 0),
        "learning_speed_scores": draw_learning_speed_scores(jax.random.fold_in(streams_of[13], 71), 0),
        "exit_switch": normal_values(streams_of[6], (REQUEST_COUNT, TOKEN_SLOTS, ALL_UNITS_WIDTH), 1.0, 6.0, ((0, 4), (1, 8))),
        "address_removal_factor": jnp.clip(jnp.exp(jax.random.uniform(streams_of[7], (ALL_UNITS_WIDTH,), jnp.float32, math.log(0.4), math.log(1.6))), 0.4, 1.6),
        "address_learning_factor": jnp.clip(jax.random.uniform(streams_of[8], (ALL_UNITS_WIDTH,), jnp.float32, 0.3, 1.5), 0.3, 1.5),
        "present_extra_factor": normal_values(streams_of[9], (ALL_UNITS_WIDTH,), 0.15, 0.9, (), jnp.float32),
        "cluster_scale_term": jnp.clip(1.0 + 0.18 * jax.random.normal(streams_of[10], (ALL_UNITS_WIDTH,), jnp.float32), 0.1, 1.9),
        "cluster_shift_term": normal_values(streams_of[11], (ALL_UNITS_WIDTH,), 0.3, 1.8, (), jnp.float32),
        "final_projection": normal_values(streams_of[12], (ALL_UNITS_WIDTH, MODEL_WIDTH), ALL_UNITS_WIDTH ** -0.5, 0.125, ((0, 32),)),
    }


DECAY_SCALE = 0.606531
UNIT_EPS = 1e-06
GROUP_EPS = 0.00064
EXACT = lax.Precision.HIGHEST

def token_step(carried, pieces, matrix_lines):
    address_removal_factor, address_learning_factor, present_extra_factor, cluster_scale_term, cluster_shift_term = matrix_lines
    acceptor_source, decay_in, key_raw, value_raw, iclr_in, switch_source, live_entries = pieces
    head_shape = (acceptor_source.shape[0], LOCAL_UNITS, PER_UNIT_WIDTH)
    acceptor_real = acceptor_source.astype(jnp.float32).reshape(head_shape)
    learn_rate = jax.nn.sigmoid(iclr_in.astype(jnp.float32))
    key_vals = key_raw.astype(jnp.float32)
    unit_dir = (key_vals * address_removal_factor).reshape(head_shape)
    unit_dir = unit_dir * lax.rsqrt(lax.optimization_barrier(jnp.sum(unit_dir * unit_dir, -1, keepdims=True)) + UNIT_EPS)
    address_scaled = (key_vals * (1.0 + (learn_rate - 1.0) * address_learning_factor) * live_entries).reshape(head_shape)
    decays = jnp.exp(-DECAY_SCALE * jax.nn.sigmoid(decay_in.astype(jnp.float32)) * live_entries).reshape(head_shape)
    payload_lines = (value_raw.astype(jnp.float32) * live_entries).reshape(head_shape)
    removal = (learn_rate * live_entries).reshape(head_shape)
    pulled = jnp.einsum('nhvk,nhk->nhv', carried, -unit_dir, precision=EXACT)
    carried = carried * decays[:, :, None, :] + pulled[..., None] * (unit_dir * removal)[:, :, None, :] + payload_lines[..., None] * address_scaled[:, :, None, :]
    wkv_out = jnp.einsum('nhvk,nhk->nhv', carried, acceptor_real, precision=EXACT)
    center = wkv_out - lax.optimization_barrier(jnp.mean(wkv_out, -1, keepdims=True))
    standardized_lines = center * lax.rsqrt(lax.optimization_barrier(jnp.mean(center * center, -1, keepdims=True)) + GROUP_EPS)
    standardized_lines = standardized_lines.reshape(acceptor_source.shape) * cluster_scale_term + cluster_shift_term
    extra_share = lax.optimization_barrier(jnp.sum(acceptor_real * address_scaled * present_extra_factor.reshape(LOCAL_UNITS, PER_UNIT_WIDTH), -1, keepdims=True)) * payload_lines
    blended_entry = ((standardized_lines + extra_share.reshape(acceptor_source.shape)) * switch_source.astype(jnp.float32) * live_entries).astype(jnp.bfloat16)
    return (carried, blended_entry)

def reference(sequence_sizes, acceptor, fading_scores, address_source, payload_source, learning_speed_scores, exit_switch, address_removal_factor, address_learning_factor, present_extra_factor, cluster_scale_term, cluster_shift_term, final_projection):
    seq_total = acceptor.shape[1]
    positions = jnp.arange(seq_total, dtype=jnp.int32)
    live_entries = (positions[:, None] < sequence_sizes.astype(jnp.int32)[None, :]).astype(jnp.float32)[..., None]
    by_token = tuple((jnp.swapaxes(tensor, 0, 1) for tensor in (acceptor, fading_scores, address_source, payload_source, learning_speed_scores, exit_switch)))
    matrix_lines = (address_removal_factor, address_learning_factor, present_extra_factor, cluster_scale_term, cluster_shift_term)
    initial = jnp.zeros((acceptor.shape[0], LOCAL_UNITS, PER_UNIT_WIDTH, PER_UNIT_WIDTH), jnp.float32)

    def advance(carried, pieces):
        return token_step(carried, pieces, matrix_lines)
    final_state, mixed_rows = lax.scan(advance, initial, by_token + (live_entries,))
    mixed_rows = jnp.swapaxes(mixed_rows, 0, 1)

    def project(row_block):
        return jnp.dot(row_block, final_projection, preferred_element_type=jnp.float32).astype(jnp.bfloat16)
    return lax.map(project, mixed_rows)
```

```python
import functools
import math

import jax
import jax.numpy as jnp
import numpy as np
from jax import lax
from jax.experimental import pallas as pl
from jax.experimental.pallas import tpu as pltpu
from jax.sharding import PartitionSpec as P

LOCAL_UNITS = 32
DECAY_SCALE = 0.606531
UNIT_EPS = 1e-06
GROUP_EPS = 0.00064
F32, BF16 = jnp.float32, jnp.bfloat16
UNIT = 64
PAIR = 128


def split2(x):
    hi = x.astype(BF16)
    return hi, (x - hi.astype(F32)).astype(BF16)


def mm(a, b):
    return jnp.dot(a, b, preferred_element_type=F32)


def mm_t(a, b):
    return lax.dot_general(a, b, (((1,), (1,)), ((), ())), preferred_element_type=F32)


def square_product(a, b):
    (ah, al), (bh, bl) = a, b
    left = jnp.concatenate([ah, al], 1)
    row = jnp.concatenate([bh, bl], 1)
    both = mm(left, jnp.concatenate([row, row], 0))
    return both[:, :PAIR] + both[:, PAIR:]


def wide_product(a, b):
    (ah, al), (bh, bl) = a, b
    both = mm(ah, jnp.concatenate([bh, bl], 1))
    return both[:, :PAIR] + both[:, PAIR:] + mm(al, bh)


def head_sum(x, ones):
    hi, lo = split2(x)
    return mm(hi, ones) + mm(lo, ones)


def sigmoid(x):
    return 1.0 / (1.0 + jnp.exp(-x))


def local_kernel(
    live_ref, acc_ref, fade_ref, key_ref, val_ref, rate_ref, rem_ref, learn_ref, extra_ref,
    tri_ref, ones_ref, level_ref, out_ref, query_ref, bonus_ref, state_ref,
):
    tokens = acc_ref.shape[0]
    half = tokens // 2
    ones = ones_ref[...]
    live = live_ref[...]
    rate = sigmoid(rate_ref[...].astype(F32))
    keys = key_ref[...].astype(F32)
    unit = keys * rem_ref[...]
    unit = unit * lax.rsqrt(head_sum(unit * unit, ones) + UNIT_EPS)
    key_mod = keys * (1.0 + (rate - 1.0) * learn_ref[...]) * live
    log_decay = -DECAY_SCALE * sigmoid(fade_ref[...].astype(F32)) * live
    values = val_ref[...] * live.astype(BF16)
    acc = acc_ref[...].astype(F32)
    bonus_ref[...] = head_sum(acc * key_mod * extra_ref[...], ones) * values.astype(F32)
    push = unit * (rate * live)

    first, rest = split2(log_decay)
    third = (log_decay - first.astype(F32) - rest.astype(F32)).astype(BF16)
    tri = tri_ref[...]
    cumul = mm(tri, first) + (mm(tri, rest) + mm(tri, third))
    middle = cumul[half - 1 : half]
    last = cumul[tokens - 1 : tokens]
    up = jnp.exp(cumul - middle)
    down = jnp.exp(middle - cumul)
    to_middle = jnp.exp(middle)
    tail = jnp.exp(last - cumul)
    read_c = acc * up
    pull_c = -unit * jnp.exp(cumul - log_decay - middle)
    push_c = split2(push * down)
    key_c = split2(key_mod * down)
    read_true = read_c * to_middle
    pull_true = pull_c * to_middle
    push_tail = (push * tail).T
    key_tail = (key_mod * tail).T
    whole_decay = jnp.exp(last)

    lane = lax.broadcasted_iota(jnp.int32, (1, PAIR), 1)
    rows = lax.broadcasted_iota(jnp.int32, (tokens, tokens), 0)
    columns = lax.broadcasted_iota(jnp.int32, (tokens, tokens), 1)
    right = jnp.concatenate([push_c[0], key_c[0]], 0)
    right_low = jnp.concatenate([push_c[1], key_c[1]], 0)
    right_twice = jnp.concatenate([right, right], 1)
    pulled_swap = pltpu.roll(pull_true, UNIT, 1)
    read_swap = pltpu.roll(read_true, UNIT, 1)
    eye = (rows[:half, :half] == columns[:half, :half]).astype(F32)
    krow = lax.broadcasted_iota(jnp.int32, (UNIT, PAIR), 0)
    klane = lax.broadcasted_iota(jnp.int32, (UNIT, PAIR), 1)
    decay_swap = pltpu.roll(whole_decay * jnp.ones((8, PAIR), F32), UNIT, 1)[:1]
    levels = level_ref.shape[0]
    outs = []
    for h in range(2):
        mine = (lane // UNIT) == h
        ph, plow = split2(jnp.where(mine, pull_c, 0.0))
        rh, rlow = split2(jnp.where(mine, read_c, 0.0))
        left = jnp.concatenate(
            [jnp.concatenate([ph, plow], 1), jnp.concatenate([rh, rlow], 1)], 0
        )
        pairs = mm_t(left, right_twice) + mm_t(jnp.concatenate([ph, rh], 0), right_low)
        a_pp = jnp.where(rows > columns, pairs[:tokens, :tokens], 0.0)
        a_pk = split2(jnp.where(rows > columns, pairs[:tokens, tokens:], 0.0))
        a_rp = split2(jnp.where(rows >= columns, pairs[tokens:, :tokens], 0.0))
        a_rk = split2(jnp.where(rows >= columns, pairs[tokens:, tokens:], 0.0))
        system_h, system_l = split2(a_pp)
        inverses = []
        for b in range(2):
            cut = slice(b * half, (b + 1) * half)
            block_h, block_l = system_h[cut, cut], system_l[cut, cut]
            inverse = eye + a_pp[cut, cut] * level_ref[0].astype(F32)
            for level in range(1, levels):
                mask = level_ref[level]
                now = split2(inverse)
                step = square_product((block_h * mask, block_l * mask), now)
                inverse = inverse + square_product(now, split2(step))
            inverses.append(split2(inverse))
        source = jnp.where(mine, mm(a_pk[0], values) + mm(a_pk[1], values), pulled_swap)
        top = square_product(inverses[0], split2(source[:half]))
        top_s = split2(top)
        below = source[half:] + square_product(
            (system_h[half:, :half], system_l[half:, :half]), top_s
        )
        bottom = square_product(inverses[1], split2(below))
        bottom_s = split2(bottom)
        removed = (
            jnp.concatenate([top_s[0], bottom_s[0]], 0),
            jnp.concatenate([top_s[1], bottom_s[1]], 0),
        )
        result = wide_product(a_rp, removed) + jnp.where(
            mine, mm(a_rk[0], values) + mm(a_rk[1], values), read_swap
        )
        outs.append(result)
        own = slice(h * UNIT, (h + 1) * UNIT)
        kt = split2(key_tail[own])
        identity = jnp.where(klane == krow + (1 - h) * UNIT, decay_swap, 0.0)
        state = wide_product(split2(push_tail[own]), removed) + jnp.where(
            mine, mm(kt[0], values) + mm(kt[1], values), identity
        )
        state_ref[h] = state if h == 0 else pltpu.roll(state, UNIT, 1)
    low = lane < UNIT
    out_ref[...] = jnp.where(low, outs[0], outs[1])
    query_ref[...] = pltpu.roll(jnp.where(low, outs[1], outs[0]), UNIT, 1)


def local_pass(live, acceptor, fading, keys, values, rates, removal, learning, extra):
    tokens, width = acceptor.shape
    half = tokens // 2
    tri = jnp.asarray(np.tril(np.ones((tokens, tokens), np.float32)), BF16)
    places = np.arange(PAIR)
    ones = jnp.asarray(places[:, None] // UNIT == places[None, :] // UNIT, BF16)
    spots = np.arange(half)
    apart = spots[:, None] ^ spots[None, :]
    levels = jnp.asarray(
        np.stack([(apart >> n) == 1 for n in range(int(math.log2(half)))]), BF16
    )
    token_block = pl.BlockSpec((tokens, PAIR), lambda i: (0, i))
    row_block = pl.BlockSpec((1, PAIR), lambda i: (0, i))

    def fixed(shape):
        return pl.BlockSpec(shape, lambda i: (0,) * len(shape))

    return pl.pallas_call(
        local_kernel,
        grid=(width // PAIR,),
        in_specs=[fixed((tokens, 1))]
        + [token_block] * 5
        + [row_block] * 3
        + [fixed(tri.shape), fixed(ones.shape), fixed(levels.shape)],
        out_specs=[token_block] * 3 + [pl.BlockSpec((2, UNIT, PAIR), lambda i: (i, 0, 0))],
        out_shape=[jax.ShapeDtypeStruct((tokens, width), F32)] * 3
        + [jax.ShapeDtypeStruct((width // UNIT, UNIT, PAIR), F32)],
        compiler_params=pltpu.CompilerParams(vmem_limit_bytes=40 * 1024 * 1024),
        cost_estimate=pl.CostEstimate(
            flops=60 * 10**9, bytes_accessed=12 * 2**20, transcendentals=3 * 10**6
        ),
    )(live, acceptor, fading, keys, values, rates, removal, learning, extra, tri, ones, levels)


def prefix_kernel(blocks, heads, map_ref, before_ref):
    lane = lax.broadcasted_iota(jnp.int32, (1, PAIR), 1)
    low = lane < UNIT
    for h in range(heads):
        before_ref[h] = jnp.zeros((UNIT, PAIR), F32)
    states = [jnp.where(low, map_ref[h], 0.0) for h in range(heads)]
    for n in range(1, blocks):
        for h in range(heads):
            before_ref[n * heads + h] = states[h]
            if n + 1 < blocks:
                step = map_ref[n * heads + h]
                transit = pltpu.roll(step, UNIT, 1)[:, :UNIT]
                states[h] = jnp.where(low, step, 0.0) + jnp.dot(
                    transit, states[h], precision=lax.Precision.HIGHEST,
                    preferred_element_type=F32,
                )


def state_before(maps, axis):
    blocks = lax.axis_size(axis)
    heads = maps.shape[0] // blocks
    mine = lax.all_to_all(maps, axis, 0, 0, tiled=True)
    before = pl.pallas_call(
        functools.partial(prefix_kernel, blocks, heads),
        out_shape=jax.ShapeDtypeStruct(mine.shape, F32),
        compiler_params=pltpu.CompilerParams(vmem_limit_bytes=24 * 1024 * 1024),
    )(mine)
    return lax.all_to_all(before, axis, 0, 0, tiled=True)


def finish_kernel(
    live_ref, out_ref, query_ref, bonus_ref, before_ref, switch_ref, gain_ref, shift_ref,
    ones_ref, row_ref,
):
    ones = ones_ref[...]
    start = jnp.concatenate([before_ref[0], pltpu.roll(before_ref[1], UNIT, 1)], 0)
    wkv = out_ref[...] + wide_product(split2(query_ref[...]), split2(start))
    center = wkv - head_sum(wkv, ones) * (1.0 / UNIT)
    spread = head_sum(center * center, ones) * (1.0 / UNIT)
    normed = center * lax.rsqrt(spread + GROUP_EPS) * gain_ref[...] + shift_ref[...]
    mixed = (normed + bonus_ref[...]) * switch_ref[...].astype(F32) * live_ref[...]
    row_ref[...] = mixed.astype(BF16)


def finish(live, out, query, bonus, before, switch, gain, shift):
    tokens, width = out.shape
    places = np.arange(PAIR)
    ones = jnp.asarray(places[:, None] // UNIT == places[None, :] // UNIT, BF16)
    token_block = pl.BlockSpec((tokens, PAIR), lambda i: (0, i))
    row_block = pl.BlockSpec((1, PAIR), lambda i: (0, i))
    return pl.pallas_call(
        finish_kernel,
        grid=(width // PAIR,),
        in_specs=[pl.BlockSpec((tokens, 1), lambda i: (0, 0))]
        + [token_block] * 3
        + [pl.BlockSpec((2, UNIT, PAIR), lambda i: (i, 0, 0)), token_block]
        + [row_block] * 2
        + [pl.BlockSpec(ones.shape, lambda i: (0, 0))],
        out_specs=token_block,
        out_shape=jax.ShapeDtypeStruct((tokens, width), BF16),
        compiler_params=pltpu.CompilerParams(vmem_limit_bytes=24 * 1024 * 1024),
    )(live, out, query, bonus, before, switch, gain, shift, ones)


def per_device(
    sequence_sizes, acceptor, fading_scores, address_source, payload_source,
    learning_speed_scores, exit_switch, address_removal_factor, address_learning_factor,
    present_extra_factor, cluster_scale_term, cluster_shift_term, final_projection,
):
    tokens = acceptor.shape[1]
    weights = lax.all_gather(final_projection, ("req", "seq"), axis=0, tiled=True)
    position = lax.axis_index("seq") * tokens + jnp.arange(tokens, dtype=jnp.int32)
    live = (position < sequence_sizes[0]).astype(F32)[:, None]
    out, query, bonus, maps = local_pass(
        live, acceptor[0], fading_scores[0], address_source[0], payload_source[0],
        learning_speed_scores[0], address_removal_factor[None], address_learning_factor[None],
        present_extra_factor[None],
    )
    before = state_before(maps, "seq")
    mixed = finish(
        live, out, query, bonus, before, exit_switch[0], cluster_scale_term[None],
        cluster_shift_term[None],
    )
    projected = jnp.dot(mixed, weights, preferred_element_type=F32)
    return projected.astype(BF16)[None]


def solution(mesh):
    tokens = P("req", "seq", None)
    placed = (P("req"),) + (tokens,) * 6 + (P(),) * 5 + (P(("req", "seq"), None),)
    return jax.shard_map(
        per_device, mesh=mesh, in_specs=placed, out_specs=tokens, check_vma=False
    )
```

```python
import functools
import math

import jax
import jax.numpy as jnp
import numpy as np
from jax import lax
from jax.experimental import pallas as pl
from jax.experimental.pallas import tpu as pltpu
from jax.sharding import PartitionSpec as P

LOCAL_UNITS = 32
DECAY_SCALE = 0.606531
UNIT_EPS = 1e-06
GROUP_EPS = 0.00064
F32, BF16 = jnp.float32, jnp.bfloat16
UNIT = 64
PAIR = 128
GROUP = 2
FINISH_GROUP = 4


def split2(x):
    hi = x.astype(BF16)
    return hi, (x - hi.astype(F32)).astype(BF16)


def mm(a, b):
    return jnp.dot(a, b, preferred_element_type=F32)


def mm_t(a, b):
    return lax.dot_general(a, b, (((1,), (1,)), ((), ())), preferred_element_type=F32)


def square_product(a, b):
    (ah, al), (bh, bl) = a, b
    left = jnp.concatenate([ah, al], 1)
    row = jnp.concatenate([bh, bl], 1)
    both = mm(left, jnp.concatenate([row, row], 0))
    return both[:, :PAIR] + both[:, PAIR:]


def wide_product(a, b):
    (ah, al), (bh, bl) = a, b
    both = mm(ah, jnp.concatenate([bh, bl], 1))
    return both[:, :PAIR] + both[:, PAIR:] + mm(al, bh)


def head_sum(x, ones):
    hi, lo = split2(x)
    return mm(hi, ones) + mm(lo, ones)


def sigmoid(x):
    return 1.0 / (1.0 + jnp.exp(-x))


def local_kernel(
    live_ref, acc_ref, fade_ref, key_ref, val_ref, rate_ref, rem_ref, learn_ref, extra_ref,
    tri_ref, ones_ref, level_ref, out_ref, query_ref, bonus_ref, state_ref,
):
    tokens = acc_ref.shape[0]
    half = tokens // 2
    ones = ones_ref[...]
    tri = tri_ref[...]
    live = live_ref[...]
    lane = lax.broadcasted_iota(jnp.int32, (1, PAIR), 1)
    low = lane < UNIT
    rows = lax.broadcasted_iota(jnp.int32, (tokens, tokens), 0)
    columns = lax.broadcasted_iota(jnp.int32, (tokens, tokens), 1)
    strict, upto = rows > columns, rows >= columns
    eye = (rows[:half, :half] == columns[:half, :half]).astype(F32)
    krow = lax.broadcasted_iota(jnp.int32, (UNIT, PAIR), 0)
    klane = lax.broadcasted_iota(jnp.int32, (UNIT, PAIR), 1)
    levels = level_ref.shape[0]
    pairs_here = acc_ref.shape[1] // PAIR
    heads = []
    for p in range(pairs_here):
        span = slice(p * PAIR, (p + 1) * PAIR)
        rate = sigmoid(rate_ref[:, span].astype(F32))
        keys = key_ref[:, span].astype(F32)
        unit = keys * rem_ref[:, span]
        unit = unit * lax.rsqrt(head_sum(unit * unit, ones) + UNIT_EPS)
        key_mod = keys * (1.0 + (rate - 1.0) * learn_ref[:, span]) * live
        log_decay = -DECAY_SCALE * sigmoid(fade_ref[:, span].astype(F32)) * live
        values = val_ref[:, span] * live.astype(BF16)
        acc = acc_ref[:, span].astype(F32)
        bonus_ref[:, span] = (
            head_sum(acc * key_mod * extra_ref[:, span], ones) * values.astype(F32)
        )
        push = unit * (rate * live)
        first, rest = split2(log_decay)
        third = (log_decay - first.astype(F32) - rest.astype(F32)).astype(BF16)
        cumul = mm(tri, first) + (mm(tri, rest) + mm(tri, third))
        middle = cumul[half - 1 : half]
        last = cumul[tokens - 1 : tokens]
        up = jnp.exp(cumul - middle)
        down = jnp.exp(middle - cumul)
        to_middle = jnp.exp(middle)
        tail = jnp.exp(last - cumul)
        read_c = acc * up
        pull_c = -unit * jnp.exp(cumul - log_decay - middle)
        push_c = split2(push * down)
        key_c = split2(key_mod * down)
        push_tail = (push * tail).T
        key_tail = (key_mod * tail).T
        whole_decay = jnp.exp(last)
        right = jnp.concatenate([push_c[0], key_c[0]], 0)
        right_low = jnp.concatenate([push_c[1], key_c[1]], 0)
        right_twice = jnp.concatenate([right, right], 1)
        pulled_swap = pltpu.roll(pull_c * to_middle, UNIT, 1)
        read_swap = pltpu.roll(read_c * to_middle, UNIT, 1)
        decay_swap = pltpu.roll(whole_decay * jnp.ones((8, PAIR), F32), UNIT, 1)[:1]
        for h in range(2):
            mine = (lane // UNIT) == h
            ph, plow = split2(jnp.where(mine, pull_c, 0.0))
            rh, rlow = split2(jnp.where(mine, read_c, 0.0))
            left = jnp.concatenate(
                [jnp.concatenate([ph, plow], 1), jnp.concatenate([rh, rlow], 1)], 0
            )
            paired = mm_t(left, right_twice) + mm_t(jnp.concatenate([ph, rh], 0), right_low)
            a_pp = jnp.where(strict, paired[:tokens, :tokens], 0.0)
            a_pk = split2(jnp.where(strict, paired[:tokens, tokens:], 0.0))
            a_rp = split2(jnp.where(upto, paired[tokens:, :tokens], 0.0))
            a_rk = split2(jnp.where(upto, paired[tokens:, tokens:], 0.0))
            own = slice(h * UNIT, (h + 1) * UNIT)
            kt = split2(key_tail[own])
            source = jnp.where(mine, mm(a_pk[0], values) + mm(a_pk[1], values), pulled_swap)
            plain = jnp.where(mine, mm(a_rk[0], values) + mm(a_rk[1], values), read_swap)
            identity = jnp.where(klane == krow + (1 - h) * UNIT, decay_swap, 0.0)
            state = jnp.where(mine, mm(kt[0], values) + mm(kt[1], values), identity)
            heads.append((a_pp, a_rp, source, plain, state, split2(push_tail[own])))
    systems = [split2(head[0]) for head in heads]
    blocks, inverses = [], []
    for (a_pp, *_), (high, small) in zip(heads, systems):
        for b in range(2):
            cut = slice(b * half, (b + 1) * half)
            blocks.append((high[cut, cut], small[cut, cut]))
            inverses.append(eye + a_pp[cut, cut] * level_ref[0].astype(F32))
    for level in range(1, levels):
        mask = level_ref[level]
        now = [split2(inverse) for inverse in inverses]
        steps = [
            square_product((high * mask, small * mask), n)
            for (high, small), n in zip(blocks, now)
        ]
        steps = [split2(step) for step in steps]
        inverses = [
            inverse + square_product(n, step) for inverse, n, step in zip(inverses, now, steps)
        ]
    inverses = [split2(inverse) for inverse in inverses]
    count = len(heads)
    tops = [
        split2(square_product(inverses[2 * i], split2(heads[i][2][:half]))) for i in range(count)
    ]
    below = [
        heads[i][2][half:]
        + square_product((systems[i][0][half:, :half], systems[i][1][half:, :half]), tops[i])
        for i in range(count)
    ]
    bottoms = [
        split2(square_product(inverses[2 * i + 1], split2(below[i]))) for i in range(count)
    ]
    outs = []
    for i in range(count):
        removed = (
            jnp.concatenate([tops[i][0], bottoms[i][0]], 0),
            jnp.concatenate([tops[i][1], bottoms[i][1]], 0),
        )
        _, a_rp, _, plain, state, push_tail = heads[i]
        outs.append(wide_product(a_rp, removed) + plain)
        state = wide_product(push_tail, removed) + state
        if i % 2:
            state = pltpu.roll(state, UNIT, 1)
        state_ref[i] = jnp.where(klane == krow + UNIT, state - 1.0, state).astype(BF16)
    for p in range(pairs_here):
        span = slice(p * PAIR, (p + 1) * PAIR)
        even, odd = outs[2 * p], outs[2 * p + 1]
        out_ref[:, span] = jnp.where(low, even, odd)
        query_ref[:, span] = pltpu.roll(jnp.where(low, odd, even), UNIT, 1)


def local_pass(live, acceptor, fading, keys, values, rates, removal, learning, extra):
    tokens, width = acceptor.shape
    half = tokens // 2
    tri = jnp.asarray(np.tril(np.ones((tokens, tokens), np.float32)), BF16)
    places = np.arange(PAIR)
    ones = jnp.asarray(places[:, None] // UNIT == places[None, :] // UNIT, BF16)
    spots = np.arange(half)
    apart = spots[:, None] ^ spots[None, :]
    levels = jnp.asarray(
        np.stack([(apart >> n) == 1 for n in range(int(math.log2(half)))]), BF16
    )
    token_block = pl.BlockSpec((tokens, GROUP * PAIR), lambda i: (0, i))
    row_block = pl.BlockSpec((1, GROUP * PAIR), lambda i: (0, i))

    def fixed(shape):
        return pl.BlockSpec(shape, lambda i: (0,) * len(shape))

    return pl.pallas_call(
        local_kernel,
        grid=(width // (GROUP * PAIR),),
        in_specs=[fixed((tokens, 1))]
        + [token_block] * 5
        + [row_block] * 3
        + [fixed(tri.shape), fixed(ones.shape), fixed(levels.shape)],
        out_specs=[token_block] * 3 + [pl.BlockSpec((2 * GROUP, UNIT, PAIR), lambda i: (i, 0, 0))],
        out_shape=[jax.ShapeDtypeStruct((tokens, width), F32)] * 3
        + [jax.ShapeDtypeStruct((width // UNIT, UNIT, PAIR), BF16)],
        compiler_params=pltpu.CompilerParams(vmem_limit_bytes=56 * 1024 * 1024),
        cost_estimate=pl.CostEstimate(
            flops=60 * 10**9, bytes_accessed=12 * 2**20, transcendentals=3 * 10**6
        ),
    )(live, acceptor, fading, keys, values, rates, removal, learning, extra, tri, ones, levels)


def prefix_kernel(blocks, heads, map_ref, before_ref):
    low = lax.broadcasted_iota(jnp.int32, (1, PAIR), 1) < UNIT
    for h in range(heads):
        before_ref[h] = jnp.zeros((UNIT, PAIR), BF16)
    states = [jnp.where(low, map_ref[h].astype(F32), 0.0) for h in range(heads)]
    for n in range(1, blocks):
        for h in range(heads):
            high, small = split2(states[h])
            before_ref[n * heads + h] = jnp.where(
                low, high.astype(F32), pltpu.roll(small.astype(F32), UNIT, 1)
            ).astype(BF16)
            if n + 1 < blocks:
                step = map_ref[n * heads + h].astype(F32)
                transit = pltpu.roll(step, UNIT, 1)[:, :UNIT].astype(BF16)
                states[h] = (
                    states[h]
                    + jnp.where(low, step, 0.0)
                    + (mm(transit, high) + mm(transit, small))
                )


def state_before(maps, axis):
    blocks = lax.axis_size(axis)
    heads = maps.shape[0] // blocks
    mine = lax.all_to_all(maps, axis, 0, 0, tiled=True)
    before = pl.pallas_call(
        functools.partial(prefix_kernel, blocks, heads),
        out_shape=jax.ShapeDtypeStruct(mine.shape, BF16),
        compiler_params=pltpu.CompilerParams(vmem_limit_bytes=24 * 1024 * 1024),
    )(mine)
    return lax.all_to_all(before, axis, 0, 0, tiled=True)


def finish_kernel(
    live_ref, out_ref, query_ref, bonus_ref, before_ref, switch_ref, gain_ref, shift_ref,
    ones_ref, row_ref,
):
    ones = ones_ref[...]
    low = lax.broadcasted_iota(jnp.int32, (1, PAIR), 1) < UNIT
    for p in range(out_ref.shape[1] // PAIR):
        span = slice(p * PAIR, (p + 1) * PAIR)
        even, odd = before_ref[2 * p].astype(F32), before_ref[2 * p + 1].astype(F32)
        even_swap, odd_swap = pltpu.roll(even, UNIT, 1), pltpu.roll(odd, UNIT, 1)
        high = jnp.concatenate([jnp.where(low, even, 0.0), jnp.where(low, 0.0, odd_swap)], 0)
        small = jnp.concatenate([jnp.where(low, even_swap, 0.0), jnp.where(low, 0.0, odd)], 0)
        wkv = out_ref[:, span] + wide_product(
            split2(query_ref[:, span]), (high.astype(BF16), small.astype(BF16))
        )
        center = wkv - head_sum(wkv, ones) * (1.0 / UNIT)
        spread = head_sum(center * center, ones) * (1.0 / UNIT)
        normed = center * lax.rsqrt(spread + GROUP_EPS) * gain_ref[:, span] + shift_ref[:, span]
        mixed = (normed + bonus_ref[:, span]) * switch_ref[:, span].astype(F32) * live_ref[...]
        row_ref[:, span] = mixed.astype(BF16)


def finish(live, out, query, bonus, before, switch, gain, shift):
    tokens, width = out.shape
    places = np.arange(PAIR)
    ones = jnp.asarray(places[:, None] // UNIT == places[None, :] // UNIT, BF16)
    token_block = pl.BlockSpec((tokens, FINISH_GROUP * PAIR), lambda i: (0, i))
    row_block = pl.BlockSpec((1, FINISH_GROUP * PAIR), lambda i: (0, i))
    return pl.pallas_call(
        finish_kernel,
        grid=(width // (FINISH_GROUP * PAIR),),
        in_specs=[pl.BlockSpec((tokens, 1), lambda i: (0, 0))]
        + [token_block] * 3
        + [pl.BlockSpec((2 * FINISH_GROUP, UNIT, PAIR), lambda i: (i, 0, 0)), token_block]
        + [row_block] * 2
        + [pl.BlockSpec(ones.shape, lambda i: (0, 0))],
        out_specs=token_block,
        out_shape=jax.ShapeDtypeStruct((tokens, width), BF16),
        compiler_params=pltpu.CompilerParams(vmem_limit_bytes=24 * 1024 * 1024),
    )(live, out, query, bonus, before, switch, gain, shift, ones)


def per_device(
    sequence_sizes, acceptor, fading_scores, address_source, payload_source,
    learning_speed_scores, exit_switch, address_removal_factor, address_learning_factor,
    present_extra_factor, cluster_scale_term, cluster_shift_term, final_projection,
):
    tokens = acceptor.shape[1]
    weights = lax.all_gather(final_projection, ("req", "seq"), axis=0, tiled=True)
    position = lax.axis_index("seq") * tokens + jnp.arange(tokens, dtype=jnp.int32)
    live = (position < sequence_sizes[0]).astype(F32)[:, None]
    out, query, bonus, maps = local_pass(
        live, acceptor[0], fading_scores[0], address_source[0], payload_source[0],
        learning_speed_scores[0], address_removal_factor[None], address_learning_factor[None],
        present_extra_factor[None],
    )
    before = state_before(maps, "seq")
    mixed = finish(
        live, out, query, bonus, before, exit_switch[0], cluster_scale_term[None],
        cluster_shift_term[None],
    )
    projected = jnp.dot(mixed, weights, preferred_element_type=F32)
    return projected.astype(BF16)[None]


def solution(mesh):
    tokens = P("req", "seq", None)
    placed = (P("req"),) + (tokens,) * 6 + (P(),) * 5 + (P(("req", "seq"), None),)
    return jax.shard_map(
        per_device, mesh=mesh, in_specs=placed, out_specs=tokens, check_vma=False
    )
```

```python
import functools
import math

import jax
import jax.numpy as jnp
import numpy as np
from jax import lax
from jax.experimental import pallas as pl
from jax.experimental.pallas import tpu as pltpu
from jax.sharding import PartitionSpec as P

LOCAL_UNITS = 32
DECAY_SCALE = 0.606531
UNIT_EPS = 1e-06
GROUP_EPS = 0.00064
F32, BF16 = jnp.float32, jnp.bfloat16
UNIT = 64
PAIR = 128
GROUP = 2
FINISH_GROUP = 4


def split2(x):
    hi = x.astype(BF16)
    return hi, (x - hi.astype(F32)).astype(BF16)


def mm(a, b):
    return jnp.dot(a, b, preferred_element_type=F32)


def mm_t(a, b):
    return lax.dot_general(a, b, (((1,), (1,)), ((), ())), preferred_element_type=F32)


def square_product(a, b):
    (ah, al), (bh, bl) = a, b
    left = jnp.concatenate([ah, al], 1)
    row = jnp.concatenate([bh, bl], 1)
    both = mm(left, jnp.concatenate([row, row], 0))
    return both[:, :PAIR] + both[:, PAIR:]


def wide_product(a, b):
    (ah, al), (bh, bl) = a, b
    both = mm(ah, jnp.concatenate([bh, bl], 1))
    return both[:, :PAIR] + both[:, PAIR:] + mm(al, bh)


def head_sum(x, ones):
    hi, lo = split2(x)
    return mm(hi, ones) + mm(lo, ones)


def sigmoid(x):
    return 1.0 / (1.0 + jnp.exp(-x))


def local_kernel(
    live_ref, acc_ref, fade_ref, key_ref, val_ref, rate_ref, rem_ref, learn_ref, extra_ref,
    tri_ref, ones_ref, level_ref, out_ref, query_ref, bonus_ref, state_ref,
):
    tokens = acc_ref.shape[0]
    half = tokens // 2
    ones = ones_ref[...]
    tri = tri_ref[...]
    live = live_ref[...]
    lane = lax.broadcasted_iota(jnp.int32, (1, PAIR), 1)
    low = lane < UNIT
    rows = lax.broadcasted_iota(jnp.int32, (tokens, tokens), 0)
    columns = lax.broadcasted_iota(jnp.int32, (tokens, tokens), 1)
    strict, upto = rows > columns, rows >= columns
    eye = (rows[:half, :half] == columns[:half, :half]).astype(F32)
    krow = lax.broadcasted_iota(jnp.int32, (UNIT, PAIR), 0)
    klane = lax.broadcasted_iota(jnp.int32, (UNIT, PAIR), 1)
    levels = level_ref.shape[0]
    pairs_here = acc_ref.shape[1] // PAIR
    heads = []
    for p in range(pairs_here):
        span = slice(p * PAIR, (p + 1) * PAIR)
        rate = sigmoid(rate_ref[:, span].astype(F32))
        keys = key_ref[:, span].astype(F32)
        unit = keys * rem_ref[:, span]
        unit = unit * lax.rsqrt(head_sum(unit * unit, ones) + UNIT_EPS)
        key_mod = keys * (1.0 + (rate - 1.0) * learn_ref[:, span]) * live
        log_decay = -DECAY_SCALE * sigmoid(fade_ref[:, span].astype(F32)) * live
        values = val_ref[:, span] * live.astype(BF16)
        acc = acc_ref[:, span].astype(F32)
        bonus_ref[:, span] = (
            head_sum(acc * key_mod * extra_ref[:, span], ones) * values.astype(F32)
        )
        push = unit * (rate * live)
        first, rest = split2(log_decay)
        third = (log_decay - first.astype(F32) - rest.astype(F32)).astype(BF16)
        cumul = mm(tri, first) + (mm(tri, rest) + mm(tri, third))
        middle = cumul[half - 1 : half]
        last = cumul[tokens - 1 : tokens]
        up = jnp.exp(cumul - middle)
        down = jnp.exp(middle - cumul)
        to_middle = jnp.exp(middle)
        tail = jnp.exp(last - cumul)
        read_c = acc * up
        pull_c = -unit * jnp.exp(cumul - log_decay - middle)
        push_c = split2(push * down)
        key_c = split2(key_mod * down)
        push_tail = (push * tail).T
        key_tail = (key_mod * tail).T
        whole_decay = jnp.exp(last)
        right = jnp.concatenate([push_c[0], key_c[0]], 0)
        right_low = jnp.concatenate([push_c[1], key_c[1]], 0)
        right_twice = jnp.concatenate([right, right], 1)
        pulled_swap = pltpu.roll(pull_c * to_middle, UNIT, 1)
        read_swap = pltpu.roll(read_c * to_middle, UNIT, 1)
        decay_swap = pltpu.roll(whole_decay * jnp.ones((8, PAIR), F32), UNIT, 1)[:1]
        for h in range(2):
            mine = (lane // UNIT) == h
            ph, plow = split2(jnp.where(mine, pull_c, 0.0))
            rh, rlow = split2(jnp.where(mine, read_c, 0.0))
            left = jnp.concatenate(
                [jnp.concatenate([ph, plow], 1), jnp.concatenate([rh, rlow], 1)], 0
            )
            paired = mm_t(left, right_twice) + mm_t(jnp.concatenate([ph, rh], 0), right_low)
            a_pp = jnp.where(strict, paired[:tokens, :tokens], 0.0)
            a_pk = split2(jnp.where(strict, paired[:tokens, tokens:], 0.0))
            a_rp = split2(jnp.where(upto, paired[tokens:, :tokens], 0.0))
            a_rk = split2(jnp.where(upto, paired[tokens:, tokens:], 0.0))
            own = slice(h * UNIT, (h + 1) * UNIT)
            kt = split2(key_tail[own])
            source = jnp.where(mine, mm(a_pk[0], values) + mm(a_pk[1], values), pulled_swap)
            plain = jnp.where(mine, mm(a_rk[0], values) + mm(a_rk[1], values), read_swap)
            identity = jnp.where(klane == krow + (1 - h) * UNIT, decay_swap, 0.0)
            state = jnp.where(mine, mm(kt[0], values) + mm(kt[1], values), identity)
            heads.append((a_pp, a_rp, source, plain, state, split2(push_tail[own])))
    systems = [split2(head[0]) for head in heads]
    blocks, inverses = [], []
    for (a_pp, *_), (high, small) in zip(heads, systems):
        for b in range(2):
            cut = slice(b * half, (b + 1) * half)
            blocks.append((high[cut, cut], small[cut, cut]))
            inverses.append(eye + a_pp[cut, cut] * level_ref[0].astype(F32))
    for level in range(1, levels):
        mask = level_ref[level]
        now = [split2(inverse) for inverse in inverses]
        steps = [
            square_product((high * mask, small * mask), n)
            for (high, small), n in zip(blocks, now)
        ]
        steps = [split2(step) for step in steps]
        inverses = [
            inverse + square_product(n, step) for inverse, n, step in zip(inverses, now, steps)
        ]
    inverses = [split2(inverse) for inverse in inverses]
    count = len(heads)
    tops = [
        split2(square_product(inverses[2 * i], split2(heads[i][2][:half]))) for i in range(count)
    ]
    below = [
        heads[i][2][half:]
        + square_product((systems[i][0][half:, :half], systems[i][1][half:, :half]), tops[i])
        for i in range(count)
    ]
    bottoms = [
        split2(square_product(inverses[2 * i + 1], split2(below[i]))) for i in range(count)
    ]
    outs = []
    for i in range(count):
        removed = (
            jnp.concatenate([tops[i][0], bottoms[i][0]], 0),
            jnp.concatenate([tops[i][1], bottoms[i][1]], 0),
        )
        _, a_rp, _, plain, state, push_tail = heads[i]
        outs.append(wide_product(a_rp, removed) + plain)
        state = wide_product(push_tail, removed) + state
        if i % 2:
            state = pltpu.roll(state, UNIT, 1)
        state_ref[i] = jnp.where(klane == krow + UNIT, state - 1.0, state).astype(BF16)
    for p in range(pairs_here):
        span = slice(p * PAIR, (p + 1) * PAIR)
        even, odd = outs[2 * p], outs[2 * p + 1]
        out_ref[:, span] = jnp.where(low, even, odd)
        query_ref[:, span] = pltpu.roll(jnp.where(low, odd, even), UNIT, 1)


def local_pass(live, acceptor, fading, keys, values, rates, removal, learning, extra):
    tokens, width = acceptor.shape
    half = tokens // 2
    tri = jnp.asarray(np.tril(np.ones((tokens, tokens), np.float32)), BF16)
    places = np.arange(PAIR)
    ones = jnp.asarray(places[:, None] // UNIT == places[None, :] // UNIT, BF16)
    spots = np.arange(half)
    apart = spots[:, None] ^ spots[None, :]
    levels = jnp.asarray(
        np.stack([(apart >> n) == 1 for n in range(int(math.log2(half)))]), BF16
    )
    token_block = pl.BlockSpec((tokens, GROUP * PAIR), lambda i: (0, i))
    row_block = pl.BlockSpec((1, GROUP * PAIR), lambda i: (0, i))

    def fixed(shape):
        return pl.BlockSpec(shape, lambda i: (0,) * len(shape))

    return pl.pallas_call(
        local_kernel,
        grid=(width // (GROUP * PAIR),),
        in_specs=[fixed((tokens, 1))]
        + [token_block] * 5
        + [row_block] * 3
        + [fixed(tri.shape), fixed(ones.shape), fixed(levels.shape)],
        out_specs=[token_block] * 3 + [pl.BlockSpec((2 * GROUP, UNIT, PAIR), lambda i: (i, 0, 0))],
        out_shape=[jax.ShapeDtypeStruct((tokens, width), F32)] * 3
        + [jax.ShapeDtypeStruct((width // UNIT, UNIT, PAIR), BF16)],
        compiler_params=pltpu.CompilerParams(vmem_limit_bytes=56 * 1024 * 1024),
        cost_estimate=pl.CostEstimate(
            flops=60 * 10**9, bytes_accessed=12 * 2**20, transcendentals=3 * 10**6
        ),
    )(live, acceptor, fading, keys, values, rates, removal, learning, extra, tri, ones, levels)


def prefix_kernel(blocks, heads, map_ref, before_ref):
    low = lax.broadcasted_iota(jnp.int32, (1, PAIR), 1) < UNIT
    for h in range(heads):
        before_ref[h] = jnp.zeros((UNIT, PAIR), BF16)
    states = [jnp.where(low, map_ref[h].astype(F32), 0.0) for h in range(heads)]
    for n in range(1, blocks):
        for h in range(heads):
            high, small = split2(states[h])
            before_ref[n * heads + h] = jnp.where(
                low, high.astype(F32), pltpu.roll(small.astype(F32), UNIT, 1)
            ).astype(BF16)
            if n + 1 < blocks:
                step = map_ref[n * heads + h].astype(F32)
                transit = pltpu.roll(step, UNIT, 1)[:, :UNIT].astype(BF16)
                states[h] = (
                    states[h]
                    + jnp.where(low, step, 0.0)
                    + (mm(transit, high) + mm(transit, small))
                )


def state_before(maps, axis):
    blocks = lax.axis_size(axis)
    heads = maps.shape[0] // blocks
    mine = lax.all_to_all(maps, axis, 0, 0, tiled=True)
    before = pl.pallas_call(
        functools.partial(prefix_kernel, blocks, heads),
        out_shape=jax.ShapeDtypeStruct(mine.shape, BF16),
        compiler_params=pltpu.CompilerParams(vmem_limit_bytes=24 * 1024 * 1024),
    )(mine)
    return lax.all_to_all(before, axis, 0, 0, tiled=True)


def finish_kernel(
    live_ref, out_ref, query_ref, bonus_ref, before_ref, switch_ref, gain_ref, shift_ref,
    ones_ref, row_ref,
):
    ones = ones_ref[...]
    low = lax.broadcasted_iota(jnp.int32, (1, PAIR), 1) < UNIT
    for p in range(out_ref.shape[1] // PAIR):
        span = slice(p * PAIR, (p + 1) * PAIR)
        even, odd = before_ref[2 * p].astype(F32), before_ref[2 * p + 1].astype(F32)
        even_swap, odd_swap = pltpu.roll(even, UNIT, 1), pltpu.roll(odd, UNIT, 1)
        high = jnp.concatenate([jnp.where(low, even, 0.0), jnp.where(low, 0.0, odd_swap)], 0)
        small = jnp.concatenate([jnp.where(low, even_swap, 0.0), jnp.where(low, 0.0, odd)], 0)
        wkv = out_ref[:, span] + wide_product(
            split2(query_ref[:, span]), (high.astype(BF16), small.astype(BF16))
        )
        center = wkv - head_sum(wkv, ones) * (1.0 / UNIT)
        spread = head_sum(center * center, ones) * (1.0 / UNIT)
        normed = center * lax.rsqrt(spread + GROUP_EPS) * gain_ref[:, span] + shift_ref[:, span]
        mixed = (normed + bonus_ref[:, span]) * switch_ref[:, span].astype(F32) * live_ref[...]
        row_ref[:, span] = mixed.astype(BF16)


def finish(live, out, query, bonus, before, switch, gain, shift):
    tokens, width = out.shape
    places = np.arange(PAIR)
    ones = jnp.asarray(places[:, None] // UNIT == places[None, :] // UNIT, BF16)
    token_block = pl.BlockSpec((tokens, FINISH_GROUP * PAIR), lambda i: (0, i))
    row_block = pl.BlockSpec((1, FINISH_GROUP * PAIR), lambda i: (0, i))
    return pl.pallas_call(
        finish_kernel,
        grid=(width // (FINISH_GROUP * PAIR),),
        in_specs=[pl.BlockSpec((tokens, 1), lambda i: (0, 0))]
        + [token_block] * 3
        + [pl.BlockSpec((2 * FINISH_GROUP, UNIT, PAIR), lambda i: (i, 0, 0)), token_block]
        + [row_block] * 2
        + [pl.BlockSpec(ones.shape, lambda i: (0, 0))],
        out_specs=token_block,
        out_shape=jax.ShapeDtypeStruct((tokens, width), BF16),
        compiler_params=pltpu.CompilerParams(vmem_limit_bytes=24 * 1024 * 1024),
    )(live, out, query, bonus, before, switch, gain, shift, ones)


def per_device(
    sequence_sizes, acceptor, fading_scores, address_source, payload_source,
    learning_speed_scores, exit_switch, address_removal_factor, address_learning_factor,
    present_extra_factor, cluster_scale_term, cluster_shift_term, final_projection,
):
    tokens = acceptor.shape[1]
    weights = [
        lax.all_gather(part, ("req", "seq"), axis=0, tiled=True)
        for part in jnp.split(final_projection, 2, 1)
    ]
    position = lax.axis_index("seq") * tokens + jnp.arange(tokens, dtype=jnp.int32)
    live = (position < sequence_sizes[0]).astype(F32)[:, None]
    out, query, bonus, maps = local_pass(
        live, acceptor[0], fading_scores[0], address_source[0], payload_source[0],
        learning_speed_scores[0], address_removal_factor[None], address_learning_factor[None],
        present_extra_factor[None],
    )
    before = state_before(maps, "seq")
    mixed = finish(
        live, out, query, bonus, before, exit_switch[0], cluster_scale_term[None],
        cluster_shift_term[None],
    )
    projected = [jnp.dot(mixed, part, preferred_element_type=F32).astype(BF16) for part in weights]
    return jnp.concatenate(projected, 1)[None]


def solution(mesh):
    tokens = P("req", "seq", None)
    placed = (P("req"),) + (tokens,) * 6 + (P(),) * 5 + (P(("req", "seq"), None),)
    return jax.shard_map(
        per_device, mesh=mesh, in_specs=placed, out_specs=tokens, check_vma=False
    )
```
